32 devices in a mesh: groups: 2 (over y), ffn: 4 (over z), hid: 4 (over x, core).
Axes of the slice: x: 2, y: 2, z: 4, core: 2. Of those that a mesh axis runs over, the one named last changes fastest.
Arguments:
- act_codes: int32 [40, 8192], P(('groups', 'ffn'), 'hid'), parts along dimension 0, may hold values from -127 to 127
- act_exps: int32 [40, 64], P(('groups', 'ffn'), 'hid'), parts along dimension 0, may hold values from -10 to -7
- gate_codes: bfloat16 [8192, 26624], P('hid', 'ffn'), may hold values from -8 to 7, as said below
- up_codes: bfloat16 [8192, 26624], P('hid', 'ffn'), may hold values from -8 to 7, as said below
- down_codes: bfloat16 [26624, 8192], P('ffn', 'hid'), may hold values from -8 to 7, as said below
- gate_scale: float32 [26624], P('ffn'), may hold values from 0.004 to 0.016
- up_scale: float32 [26624], P('ffn'), may hold values from 0.004 to 0.016
- down_scale: float32 [8192], P('hid'), may hold values from 0.0015 to 0.006
Outputs:
- layer_out: bfloat16 [40, 8192], P(('groups', 'ffn'), 'hid'), parts along dimension 0
The draws below stay inside these ranges and needn't reach their ends.
There are 2 independent parts, one for each index of `groups`. The reference program is written for one: setup_inputs(seed, part) draws one part's arguments, and reference() takes and returns one part's arrays. A program takes and returns all parts, laid end to end along the dimension named above; an argument that names none is the same for every part. Nothing has to cross between parts.
Inputs may be any that keep to these rules, and one draw needn't show every extreme that they name: `gate_codes`: integer levels. `up_codes`: integer levels. `down_codes`: integer levels.
All inputs are finite; a program needn't handle non-finite values.
Results may differ from the reference program's by a relative error of at most 0.0058.
Values may be sent and summed in bfloat16 or wider, within the bound.
A program may use at most 192 MiB of HBM per device.

```python
import math
import jax
import jax.numpy as jnp
import numpy as np
from jax import lax

D = 8192
FF = 26624
BLOCK = 128
TOKENS = 20


def draw_gate_codes(key, part):
    key = jax.random.fold_in(key, 11)
    return jax.random.randint(key, (D, FF), -8, 8).astype(jnp.float32).astype(jnp.bfloat16)


def draw_up_codes(key, part):
    key = jax.random.fold_in(key, 23)
    return jax.random.randint(key, (D, FF), -8, 8).astype(jnp.float32).astype(jnp.bfloat16)


def draw_down_codes(key, part):
    key = jax.random.fold_in(key, 37)
    return jax.random.randint(key, (FF, D), -8, 8).astype(jnp.float32).astype(jnp.bfloat16)


def plant(result, stream_key, smallest, largest):
    shape = result.shape
    index_at = [jax.random.randint(jax.random.fold_in(stream_key, axis), (), 0, shape[axis]) for axis in range(len(shape))]
    result = result.at[tuple(index_at)].set(smallest)
    longest = shape.index(max(shape))
    index_at[longest] = (index_at[longest] + 1) % shape[longest]
    return result.at[tuple(index_at)].set(largest)


def steps_of(rng, extent, pieces, least, high):
    def one(position, parts):
        steps = jax.random.uniform(jax.random.fold_in(jax.random.fold_in(rng, 6), position), (parts,), jnp.float32, least / len(pieces), high / len(pieces))
        return jnp.repeat(jnp.exp(steps), extent[position] // parts).reshape((-1,) + (1,) * (len(extent) - position - 1))

    gain = one(*pieces[0])
    for cut in pieces[1:]:
        gain = gain * one(*cut)
    return gain


def setup_inputs(seed: int = 0, part: int = 0) -> dict:
    key_list = jax.random.split(jax.random.key(seed), 9)
    part_splits = jax.random.split(jax.random.fold_in(key_list[8], part), 9)
    return {
        "act_codes": plant(jax.random.randint(part_splits[0], (TOKENS, D), -127, 128), jax.random.fold_in(part_splits[0], 1), -127, 127).astype(jnp.int32),
        "act_exps": plant(jax.random.randint(part_splits[1], (TOKENS, D // BLOCK), -10, -6), jax.random.fold_in(part_splits[1], 1), -10, (-6) - 1).astype(jnp.int32),
        "gate_codes": draw_gate_codes(jax.random.fold_in(key_list[8], 71), part),
        "up_codes": draw_up_codes(jax.random.fold_in(key_list[8], 71), part),
        "down_codes": draw_down_codes(jax.random.fold_in(key_list[8], 71), part),
        "gate_scale": jnp.clip(jnp.exp(math.log(0.016) - 1.3862944 * jax.random.uniform(key_list[5], (FF,), jnp.float32) ** steps_of(key_list[5], (FF,), ((0, 4),), -0.2, 0.2)), 0.004, 0.016),
        "up_scale": jnp.clip(jnp.exp(math.log(0.016) - 1.3862944 * jax.random.uniform(key_list[6], (FF,), jnp.float32) ** steps_of(key_list[6], (FF,), ((0, 4),), -0.2, 0.2)), 0.004, 0.016),
        "down_scale": jnp.clip(jnp.exp(math.log(0.006) - 1.3862944 * jax.random.uniform(key_list[7], (D,), jnp.float32) ** steps_of(key_list[7], (D,), ((0, 4),), -0.2, 0.2)), 0.0015, 0.006),
    }


def field_product(first, second):
    return ((first[0] * second[0] + 2 * first[1] * second[1]) % 5, (first[0] * second[1] + first[1] * second[0]) % 5)

def paley_table():
    elements = [(alpha, beta) for alpha in range(5) for beta in range(5)]
    squares = set()
    for item in elements:
        if item != (0, 0):
            squares.add(field_product(item, item))
    jacobi = np.zeros((25, 25))
    for left in range(25):
        for right in range(25):
            diff = ((elements[left][0] - elements[right][0]) % 5, (elements[left][1] - elements[right][1]) % 5)
            if diff == (0, 0):
                jacobi[left, right] = 0.0
            elif diff in squares:
                jacobi[left, right] = 1.0
            else:
                jacobi[left, right] = -1.0
    conference = np.zeros((26, 26))
    conference[0, 1:] = 1.0
    conference[1:, 0] = 1.0
    conference[1:, 1:] = jacobi
    return np.kron(conference, np.array([[1.0, -1.0], [-1.0, -1.0]])) + np.kron(np.eye(26), np.array([[1.0, 1.0], [1.0, -1.0]]))

def sylvester_table(order):
    table = np.ones((1, 1))
    while table.shape[0] < order:
        table = np.kron(table, np.array([[1.0, 1.0], [1.0, -1.0]]))
    return table

def reference(act_codes, act_exps, gate_codes, up_codes, down_codes, gate_scale, up_scale, down_scale):
    blocks = D // BLOCK
    scales = jnp.exp2(act_exps.astype(jnp.float32))
    features = (act_codes.reshape(TOKENS, blocks, BLOCK).astype(jnp.float32) * scales[:, :, None]).reshape(TOKENS, D).astype(jnp.bfloat16)
    gate = jnp.dot(features, gate_codes, preferred_element_type=jnp.float32) * gate_scale
    up_val = jnp.dot(features, up_codes, preferred_element_type=jnp.float32) * up_scale
    hidden = (jax.nn.silu(gate) * up_val).astype(jnp.bfloat16)
    outer = FF // 52
    small_table = jnp.asarray(paley_table(), dtype=jnp.bfloat16)
    big_table = jnp.asarray(sylvester_table(outer), dtype=jnp.float32)
    cube = hidden.reshape(TOKENS, outer, 52)
    mixed = jnp.einsum('tji,ik->tjk', cube, small_table, preferred_element_type=jnp.float32)
    turned = jnp.einsum('tjk,jl->tlk', mixed, big_table, precision=lax.Precision.HIGHEST)
    rotated = (turned * (1.0 / np.sqrt(FF))).reshape(TOKENS, FF).astype(jnp.bfloat16)
    total = jnp.dot(rotated, down_codes, preferred_element_type=jnp.float32)
    return (total * down_scale).astype(jnp.bfloat16)
```

```python
import functools

import jax
import jax.numpy as jnp
import numpy as np
from jax import lax
from jax.experimental import pallas as pl
from jax.experimental.pallas import tpu as pltpu
from jax.sharding import PartitionSpec as P

MESH = pl.DeviceIdType.MESH


def field_product(first, second):
    return (
        (first[0] * second[0] + 2 * first[1] * second[1]) % 5,
        (first[0] * second[1] + first[1] * second[0]) % 5,
    )


def paley_table():
    elements = [(alpha, beta) for alpha in range(5) for beta in range(5)]
    squares = set()
    for item in elements:
        if item != (0, 0):
            squares.add(field_product(item, item))
    jacobi = np.zeros((25, 25))
    for left in range(25):
        for right in range(25):
            diff = (
                (elements[left][0] - elements[right][0]) % 5,
                (elements[left][1] - elements[right][1]) % 5,
            )
            if diff == (0, 0):
                jacobi[left, right] = 0.0
            elif diff in squares:
                jacobi[left, right] = 1.0
            else:
                jacobi[left, right] = -1.0
    conference = np.zeros((26, 26))
    conference[0, 1:] = 1.0
    conference[1:, 0] = 1.0
    conference[1:, 1:] = jacobi
    return np.kron(conference, np.array([[1.0, -1.0], [-1.0, -1.0]])) + np.kron(
        np.eye(26), np.array([[1.0, 1.0], [1.0, -1.0]])
    )


def sylvester_table(order):
    table = np.ones((1, 1))
    while table.shape[0] < order:
        table = np.kron(table, np.array([[1.0, 1.0], [1.0, -1.0]]))
    return table


def activate(sums, gate_scale, up_scale, width):
    gate = sums[:, :width] * gate_scale
    up_val = sums[:, width:] * up_scale
    return (jax.nn.silu(gate) * up_val).astype(jnp.bfloat16)


def on_device(
    act_codes, act_exps, gate_codes, up_codes, down_codes, gate_scale, up_scale, down_scale
):
    row_count, col_count = act_codes.shape
    blocks = act_exps.shape[1]
    scales = jnp.exp2(act_exps.astype(jnp.float32))
    features = (
        (
            act_codes.reshape(row_count, blocks, col_count // blocks).astype(jnp.float32)
            * scales[:, :, None]
        )
        .reshape(row_count, col_count)
        .astype(jnp.bfloat16)
    )
    width = gate_codes.shape[1]
    piece = lax.all_gather(features, "ffn", axis=0, tiled=True)
    gate_part = jnp.dot(piece, gate_codes, preferred_element_type=jnp.float32)
    up_part = jnp.dot(piece, up_codes, preferred_element_type=jnp.float32)
    partial_sums = jnp.concatenate([gate_part, up_part], axis=1)
    summed = lax.psum(partial_sums, "hid")
    hidden = activate(summed, gate_scale, up_scale, width)
    parts = lax.axis_size("ffn")
    tokens = hidden.shape[0]
    per_dev = tokens // parts
    local = width // 52
    small_table = jnp.asarray(paley_table(), dtype=jnp.bfloat16)
    outer_table = jnp.asarray(sylvester_table(parts), dtype=jnp.float32)
    inner_table = jnp.asarray(sylvester_table(local), dtype=jnp.float32)
    norm_factor = 1.0 / np.sqrt(parts * width)
    grouped = hidden.reshape(parts, per_dev, width)
    block = lax.all_to_all(grouped, "ffn", split_axis=0, concat_axis=0, tiled=True)
    items = block.shape[1]
    cube = block.reshape(parts, items, local, 52)
    mixed = jnp.einsum("snli,ik->snlk", cube, small_table, preferred_element_type=jnp.float32)
    across = jnp.einsum("snlk,sS->Snlk", mixed, outer_table, precision=lax.Precision.HIGHEST)
    turned = jnp.einsum("Snlk,lL->SnLk", across, inner_table, precision=lax.Precision.HIGHEST)
    rotated = (turned * norm_factor).reshape(parts, items, width).astype(jnp.bfloat16)
    returned = lax.all_to_all(rotated, "ffn", split_axis=0, concat_axis=0, tiled=True)
    rotated_rows = returned.reshape(tokens, width)
    total = lax.psum_scatter(
        jnp.dot(rotated_rows, down_codes, preferred_element_type=jnp.float32),
        "ffn",
        scatter_dimension=0,
        tiled=True,
    )
    return (total * down_scale).astype(jnp.bfloat16)


LANES = 128
ORDER = 52
SPLIT = 4
TILE_ROWS = 512
RING = 10
PAD = 24
FULL = 32


def flip(index, mask):
    if mask == 1:
        return index + 1 - 2 * (index % 2)
    if mask == 2:
        return (index + 2) % 4
    if mask == 3:
        return 3 - index
    return index


def sign_of(first, second):
    low = (first % 2) * (second % 2)
    high = (first // 2) * (second // 2)
    odd = (low + high) % 2
    return jnp.asarray(1 - 2 * odd, jnp.int32).astype(jnp.float32)


def cut_chunk(blocks):
    cuts = []
    while blocks > 5:
        cuts.append(4)
        blocks -= 4
    if blocks > 2:
        cuts += [blocks - 2, 2]
    else:
        cuts.append(blocks)
    return cuts


def layer_kernel(plan, *refs):
    rows, depth, width, feats, norm = plan
    chunk = width // SPLIT
    cuts = [blocks * LANES for blocks in cut_chunk(chunk // LANES)]
    starts = [sum(cuts[:index]) for index in range(len(cuts))]
    count = len(cuts)
    tokens = rows * SPLIT
    blocks = depth // LANES
    down_tiles = width // TILE_ROWS
    refs = list(refs)
    (codes, exps, gate_hbm, up_hbm, down_hbm, gscale, uscale, dscale, table_hbm, out) = refs[:10]
    (ring, table, down, gs, us, fold, xrecv, xfull, xmat, zsum, zall, rot, part, obuf, orecv) = refs[10:25]
    psend = refs[25 : 25 + count]
    precv = refs[25 + count : 25 + 2 * count]
    hall = refs[25 + 2 * count : 25 + 3 * count]
    (ring_sem, table_sem, down_sem, scale_sem, xs, xr, ps, pr, hs, hr, zs, zr, os, orr) = refs[25 + 3 * count :]
    me_f = lax.axis_index("ffn")
    me_h = lax.axis_index("hid")

    masks = (2, 3, 1, 0)
    units = []
    for sub in range(count):
        for mask in masks:
            units.append((sub, mask, 0))
            units.append((sub, mask, 1))

    def unit_copy(index):
        sub, mask, which = units[index]
        source = up_hbm if which else gate_hbm
        slot = index % RING
        at = pl.multiple_of(flip(me_h, mask) * chunk + starts[sub], LANES)
        return pltpu.make_async_copy(
            source.at[:, pl.ds(at, cuts[sub])],
            ring.at[slot, :, pl.ds(0, cuts[sub])],
            ring_sem.at[slot],
        )

    def down_copy(index):
        piece = pl.ds(index * TILE_ROWS, TILE_ROWS)
        return pltpu.make_async_copy(down_hbm.at[piece, :], down.at[piece, :], down_sem.at[index])

    def table_copy(sub):
        piece = pl.ds(starts[sub], cuts[sub])
        return pltpu.make_async_copy(table_hbm.at[piece, :], table.at[piece, :], table_sem.at[sub])

    def scale_copy(which):
        source, target = ((gscale, gs), (uscale, us))[which]
        at = pl.multiple_of(me_h * chunk, LANES)
        return pltpu.make_async_copy(source.at[:, pl.ds(at, chunk)], target, scale_sem.at[which])

    for which in range(2):
        scale_copy(which).start()
    for index in range(min(RING, len(units))):
        unit_copy(index).start()
    for sub in range(count):
        table_copy(sub).start()

    barrier = pltpu.get_barrier_semaphore()
    for mask in (1, 2, 3):
        pl.semaphore_signal(barrier, inc=1, device_id={"ffn": flip(me_f, mask)}, device_id_type=MESH)
        pl.semaphore_signal(barrier, inc=1, device_id={"hid": flip(me_h, mask)}, device_id_type=MESH)

    powers = lax.shift_left(jnp.ones_like(exps[...]), exps[...] + 10).astype(jnp.float32) * (2.0**-10)
    for block in range(blocks):
        at = block * LANES
        scale = powers[:, at // feats : at // feats + 1]
        fold[0, pl.ds(block * rows, rows), :] = codes[:, pl.ds(at, LANES)].astype(jnp.float32) * scale
    xrecv[0] = fold[0].astype(jnp.bfloat16)
    pl.semaphore_wait(barrier, 6)

    def feat_copy(mask):
        return pltpu.make_async_remote_copy(
            src_ref=xrecv.at[0], dst_ref=xrecv.at[mask], send_sem=xs.at[mask - 1], recv_sem=xr.at[mask - 1],
            device_id={"ffn": flip(me_f, mask)}, device_id_type=MESH,
        )

    for mask in (3, 2, 1):
        feat_copy(mask).start()
    xfull[...] = jnp.zeros_like(xfull)
    for mask in (1, 2, 3):
        feat_copy(mask).wait_recv()
    for mask in range(4):
        fold[flip(me_f, mask)] = xrecv[mask].astype(jnp.float32)
    for owner in range(SPLIT):
        for block in range(blocks):
            xfull[pl.ds(owner * rows, rows), pl.ds(block * LANES, LANES)] = fold[owner, pl.ds(block * rows, rows), :]
    xmat[...] = xfull[...].astype(jnp.bfloat16)

    def part_copy(sub, mask):
        return pltpu.make_async_remote_copy(
            src_ref=psend[sub].at[mask], dst_ref=precv[sub].at[mask - 1],
            send_sem=ps.at[sub * 3 + mask - 1], recv_sem=pr.at[sub * 3 + mask - 1],
            device_id={"hid": flip(me_h, mask)}, device_id_type=MESH,
        )

    def hidden_copy(sub, mask):
        return pltpu.make_async_remote_copy(
            src_ref=hall[sub].at[0], dst_ref=hall[sub].at[mask],
            send_sem=hs.at[sub * 3 + mask - 1], recv_sem=hr.at[sub * 3 + mask - 1],
            device_id={"ffn": flip(me_f, mask)}, device_id_type=MESH,
        )

    def z_copy(mask):
        return pltpu.make_async_remote_copy(
            src_ref=zall.at[0], dst_ref=zall.at[mask], send_sem=zs.at[mask - 1], recv_sem=zr.at[mask - 1],
            device_id={"hid": flip(me_h, mask)}, device_id_type=MESH,
        )

    def out_copy(mask):
        return pltpu.make_async_remote_copy(
            src_ref=obuf.at[flip(me_f, mask)], dst_ref=orecv.at[mask - 1],
            send_sem=os.at[mask - 1], recv_sem=orr.at[mask - 1],
            device_id={"ffn": flip(me_f, mask)}, device_id_type=MESH,
        )

    def finish_hidden(sub):
        if sub == 0:
            for which in range(2):
                scale_copy(which).wait()
        for mask in (1, 2, 3):
            part_copy(sub, mask).wait_recv()
        piece = pl.ds(starts[sub], cuts[sub])
        sums = []
        for which in range(2):
            total = psend[sub][0, which]
            for mask in (1, 2, 3):
                total = total + precv[sub][mask - 1, which]
            sums.append(total)
        gate = sums[0] * gs[:, piece]
        value = gate / (1.0 + jnp.exp(-gate)) * (sums[1] * us[:, piece])
        padded = jnp.concatenate([value, jnp.zeros((FULL - PAD, cuts[sub]), jnp.float32)], axis=0)
        hall[sub][0] = padded.astype(jnp.bfloat16)
        for mask in (3, 2, 1):
            hidden_copy(sub, mask).start()

    def mix(sub):
        table_copy(sub).wait()
        total = hall[sub][0].astype(jnp.float32) * sign_of(me_f, me_f)
        for mask in (1, 2, 3):
            hidden_copy(sub, mask).wait_recv()
            total = total + hall[sub][mask].astype(jnp.float32) * sign_of(flip(me_f, mask), me_f)
        total = total[:PAD]
        high = total.astype(jnp.bfloat16).astype(jnp.float32)
        both = jnp.concatenate([high, total - high], axis=0).astype(jnp.bfloat16)
        mixed = jnp.dot(both, table[pl.ds(starts[sub], cuts[sub]), :], preferred_element_type=jnp.float32)
        mixed = mixed[:PAD] + mixed[PAD:]
        if sub == 0:
            zsum[...] = mixed
        else:
            zsum[...] += mixed

    down_next = 0
    for index, (sub, mask, which) in enumerate(units):
        unit_copy(index).wait()
        slot = index % RING
        value = jnp.dot(xmat[...], ring[slot, :, pl.ds(0, cuts[sub])], preferred_element_type=jnp.float32)
        psend[sub][mask, which] = value[:PAD]
        if index + RING < len(units):
            unit_copy(index + RING).start()
        elif down_next < down_tiles:
            down_copy(down_next).start()
            down_next += 1
        if which == 1:
            if mask != 0:
                part_copy(sub, mask).start()
            if mask == 3 and sub >= 1:
                finish_hidden(sub - 1)
            if mask == 0 and sub >= 1:
                mix(sub - 1)
    while down_next < down_tiles:
        down_copy(down_next).start()
        down_next += 1
    finish_hidden(count - 1)
    mix(count - 1)

    padded = jnp.concatenate([zsum[...], jnp.zeros((FULL - PAD, chunk), jnp.float32)], axis=0)
    zall[0] = padded.astype(jnp.bfloat16)
    for mask in (3, 2, 1):
        z_copy(mask).start()
    for index in range(down_tiles):
        down_copy(index).wait()
    for mask in (1, 2, 3):
        z_copy(mask).wait_recv()
    for target in range(SPLIT):
        total = zall[0].astype(jnp.float32) * (sign_of(me_h, target) * norm)
        for mask in (1, 2, 3):
            total = total + zall[mask].astype(jnp.float32) * (sign_of(flip(me_h, mask), target) * norm)
        rot[target] = total.astype(jnp.bfloat16)

    @pl.loop(0, depth // 512)
    def _(tile):
        at = pl.ds(pl.multiple_of(tile * 512, 512), 512)
        total = jnp.zeros((FULL, 512), jnp.float32)
        for target in range(SPLIT):
            total = total + jnp.dot(
                rot[target], down[pl.ds(target * chunk, chunk), at], preferred_element_type=jnp.float32
            )
        part[:, at] = total

    for owner in range(SPLIT):
        for block in range(blocks):
            fold[owner, pl.ds(block * rows, rows), :] = part[pl.ds(owner * rows, rows), pl.ds(block * LANES, LANES)]
    obuf[...] = fold[...].astype(jnp.bfloat16)
    for mask in (3, 2, 1):
        out_copy(mask).start()
    total = fold[me_f]
    for mask in (1, 2, 3):
        out_copy(mask).wait_recv()
        total = total + orecv[mask - 1].astype(jnp.float32)
    fold[0] = total
    for block in range(blocks):
        at = pl.ds(block * LANES, LANES)
        out[:, at] = (fold[0, pl.ds(block * rows, rows), :] * dscale[:, at]).astype(jnp.bfloat16)

    for mask in (1, 2, 3):
        feat_copy(mask).wait_send()
        z_copy(mask).wait_send()
        out_copy(mask).wait_send()
        for sub in range(count):
            part_copy(sub, mask).wait_send()
            hidden_copy(sub, mask).wait_send()


def fused_on_device(
    act_codes, act_exps, gate_codes, up_codes, down_codes, gate_scale, up_scale, down_scale
):
    rows, depth = act_codes.shape
    width = gate_codes.shape[1]
    chunk = width // SPLIT
    feats = depth // act_exps.shape[1]
    cuts = [blocks * LANES for blocks in cut_chunk(chunk // LANES)]
    count = len(cuts)
    norm = float(1.0 / np.sqrt(width * lax.axis_size("ffn")))
    table = jnp.asarray(
        np.kron(sylvester_table(chunk // ORDER), paley_table()).astype(np.float32), dtype=jnp.bfloat16
    )
    folded = rows * (depth // LANES)
    vmem = pl.BlockSpec(memory_space=pltpu.VMEM)
    hbm = pl.BlockSpec(memory_space=pl.ANY)
    f32, bf16 = jnp.float32, jnp.bfloat16
    scratch = [
        pltpu.VMEM((RING, depth, max(cuts)), bf16),
        pltpu.VMEM((chunk, chunk), bf16),
        pltpu.VMEM((width, depth), bf16),
        pltpu.VMEM((1, chunk), f32),
        pltpu.VMEM((1, chunk), f32),
        pltpu.VMEM((SPLIT, folded, LANES), f32),
        pltpu.VMEM((SPLIT, folded, LANES), bf16),
        pltpu.VMEM((FULL, depth), f32),
        pltpu.VMEM((FULL, depth), bf16),
        pltpu.VMEM((PAD, chunk), f32),
        pltpu.VMEM((SPLIT, FULL, chunk), bf16),
        pltpu.VMEM((SPLIT, FULL, chunk), bf16),
        pltpu.VMEM((FULL, depth), f32),
        pltpu.VMEM((SPLIT, folded, LANES), bf16),
        pltpu.VMEM((SPLIT - 1, folded, LANES), bf16),
    ]
    scratch += [pltpu.VMEM((SPLIT, 2, PAD, cut), f32) for cut in cuts]
    scratch += [pltpu.VMEM((SPLIT - 1, 2, PAD, cut), f32) for cut in cuts]
    scratch += [pltpu.VMEM((SPLIT, FULL, cut), bf16) for cut in cuts]
    dma = pltpu.SemaphoreType.DMA
    scratch += [dma((RING,)), dma((count,)), dma((width // TILE_ROWS,)), dma((2,)), dma((3,)), dma((3,))]
    scratch += [dma((3 * count,)) for _ in range(4)]
    scratch += [dma((3,)) for _ in range(4)]
    return pl.pallas_call(
        functools.partial(layer_kernel, (rows, depth, width, feats, norm)),
        out_shape=jax.ShapeDtypeStruct((rows, depth), bf16),
        in_specs=[vmem, vmem, hbm, hbm, hbm, hbm, hbm, vmem, hbm],
        out_specs=vmem,
        scratch_shapes=scratch,
        compiler_params=pltpu.CompilerParams(
            collective_id=0, has_side_effects=True, vmem_limit_bytes=62 * 2**20
        ),
        cost_estimate=pl.CostEstimate(
            flops=6 * rows * SPLIT * depth * width, bytes_accessed=6 * depth * width, transcendentals=0
        ),
    )(
        act_codes, act_exps, gate_codes, up_codes, down_codes,
        gate_scale.reshape(1, width), up_scale.reshape(1, width), down_scale.reshape(1, depth), table,
    )


def solution(mesh):
    in_specs = (
        P(("groups", "ffn"), "hid"),
        P(("groups", "ffn"), "hid"),
        P("hid", "ffn"),
        P("hid", "ffn"),
        P("ffn", "hid"),
        P("ffn"),
        P("ffn"),
        P("hid"),
    )
    out_specs = P(("groups", "ffn"), "hid")
    square = mesh.shape["ffn"] == SPLIT and mesh.shape["hid"] == SPLIT
    return jax.shard_map(
        fused_on_device if square else on_device, mesh=mesh, in_specs=in_specs, out_specs=out_specs, check_vma=False
    )
```

```python
import functools

import jax
import jax.numpy as jnp
import numpy as np
from jax import lax
from jax.experimental import pallas as pl
from jax.experimental.pallas import tpu as pltpu
from jax.sharding import PartitionSpec as P

MESH = pl.DeviceIdType.MESH


def field_product(first, second):
    return (
        (first[0] * second[0] + 2 * first[1] * second[1]) % 5,
        (first[0] * second[1] + first[1] * second[0]) % 5,
    )


def paley_table():
    elements = [(alpha, beta) for alpha in range(5) for beta in range(5)]
    squares = set()
    for item in elements:
        if item != (0, 0):
            squares.add(field_product(item, item))
    jacobi = np.zeros((25, 25))
    for left in range(25):
        for right in range(25):
            diff = (
                (elements[left][0] - elements[right][0]) % 5,
                (elements[left][1] - elements[right][1]) % 5,
            )
            if diff == (0, 0):
                jacobi[left, right] = 0.0
            elif diff in squares:
                jacobi[left, right] = 1.0
            else:
                jacobi[left, right] = -1.0
    conference = np.zeros((26, 26))
    conference[0, 1:] = 1.0
    conference[1:, 0] = 1.0
    conference[1:, 1:] = jacobi
    return np.kron(conference, np.array([[1.0, -1.0], [-1.0, -1.0]])) + np.kron(
        np.eye(26), np.array([[1.0, 1.0], [1.0, -1.0]])
    )


def sylvester_table(order):
    table = np.ones((1, 1))
    while table.shape[0] < order:
        table = np.kron(table, np.array([[1.0, 1.0], [1.0, -1.0]]))
    return table


def activate(sums, gate_scale, up_scale, width):
    gate = sums[:, :width] * gate_scale
    up_val = sums[:, width:] * up_scale
    return (jax.nn.silu(gate) * up_val).astype(jnp.bfloat16)


def on_device(
    act_codes, act_exps, gate_codes, up_codes, down_codes, gate_scale, up_scale, down_scale
):
    row_count, col_count = act_codes.shape
    blocks = act_exps.shape[1]
    scales = jnp.exp2(act_exps.astype(jnp.float32))
    features = (
        (
            act_codes.reshape(row_count, blocks, col_count // blocks).astype(jnp.float32)
            * scales[:, :, None]
        )
        .reshape(row_count, col_count)
        .astype(jnp.bfloat16)
    )
    width = gate_codes.shape[1]
    piece = lax.all_gather(features, "ffn", axis=0, tiled=True)
    gate_part = jnp.dot(piece, gate_codes, preferred_element_type=jnp.float32)
    up_part = jnp.dot(piece, up_codes, preferred_element_type=jnp.float32)
    partial_sums = jnp.concatenate([gate_part, up_part], axis=1)
    summed = lax.psum(partial_sums, "hid")
    hidden = activate(summed, gate_scale, up_scale, width)
    parts = lax.axis_size("ffn")
    tokens = hidden.shape[0]
    per_dev = tokens // parts
    local = width // 52
    small_table = jnp.asarray(paley_table(), dtype=jnp.bfloat16)
    outer_table = jnp.asarray(sylvester_table(parts), dtype=jnp.float32)
    inner_table = jnp.asarray(sylvester_table(local), dtype=jnp.float32)
    norm_factor = 1.0 / np.sqrt(parts * width)
    grouped = hidden.reshape(parts, per_dev, width)
    block = lax.all_to_all(grouped, "ffn", split_axis=0, concat_axis=0, tiled=True)
    items = block.shape[1]
    cube = block.reshape(parts, items, local, 52)
    mixed = jnp.einsum("snli,ik->snlk", cube, small_table, preferred_element_type=jnp.float32)
    across = jnp.einsum("snlk,sS->Snlk", mixed, outer_table, precision=lax.Precision.HIGHEST)
    turned = jnp.einsum("Snlk,lL->SnLk", across, inner_table, precision=lax.Precision.HIGHEST)
    rotated = (turned * norm_factor).reshape(parts, items, width).astype(jnp.bfloat16)
    returned = lax.all_to_all(rotated, "ffn", split_axis=0, concat_axis=0, tiled=True)
    rotated_rows = returned.reshape(tokens, width)
    total = lax.psum_scatter(
        jnp.dot(rotated_rows, down_codes, preferred_element_type=jnp.float32),
        "ffn",
        scatter_dimension=0,
        tiled=True,
    )
    return (total * down_scale).astype(jnp.bfloat16)


LANES = 128
ORDER = 52
SPLIT = 4
TILE_ROWS = 256
GROUPS = 2
RING = 12
PAD = 24
FULL = 32


def flip(index, mask):
    if mask == 1:
        return index + 1 - 2 * (index % 2)
    if mask == 2:
        return (index + 2) % 4
    if mask == 3:
        return 3 - index
    return index


def sign_of(first, second):
    low = (first % 2) * (second % 2)
    high = (first // 2) * (second // 2)
    odd = (low + high) % 2
    return jnp.asarray(1 - 2 * odd, jnp.int32).astype(jnp.float32)


def cut_chunk(blocks):
    cuts = []
    while blocks > 5:
        cuts.append(4)
        blocks -= 4
    if blocks > 2:
        cuts += [blocks - 2, 2]
    else:
        cuts.append(blocks)
    return cuts


def layer_kernel(plan, *refs):
    rows, depth, width, feats, norm = plan
    chunk = width // SPLIT
    cuts = [blocks * LANES for blocks in cut_chunk(chunk // LANES)]
    starts = [sum(cuts[:index]) for index in range(len(cuts))]
    count = len(cuts)
    blocks = depth // LANES
    half = width // GROUPS
    down_tiles = half // TILE_ROWS
    refs = list(refs)
    (codes, exps, gate_hbm, up_hbm, down_hbm, scales, dscale, table_hbm, out) = refs[:9]
    (table, down, fold, xrecv, xfull, xmat, zsum, zpair, zall, rot, part, obuf, orecv) = refs[9:22]
    weights, own, psend, precv, xsend, xgot, hall = [refs[22 + count * k : 22 + count * (k + 1)] for k in range(7)]
    (unit_sem, table_sem, down_sem, fs, fr, ps, pr, cs, cr, hs, hr, ys, yr, zs, zr, os, orr) = refs[22 + 7 * count :]
    me_g = lax.axis_index("groups")
    me_f = lax.axis_index("ffn")
    me_h = lax.axis_index("hid")
    me_x, me_c = me_h // 2, me_h % 2
    others = [(across, mask) for across in (1, 0) for mask in (3, 2, 1, 0) if across or mask]

    def token_peer(across, mask):
        return {"groups": (me_g + across) % 2, "ffn": flip(me_f, mask)}

    units = [(sub, other, which) for sub in range(count) for other in (1, 0) for which in (0, 1)]

    def unit_copy(index):
        sub, other, which = units[index]
        source = up_hbm if which else gate_hbm
        at = pl.multiple_of((2 * me_g + (me_c + other) % 2) * chunk + starts[sub], LANES)
        return pltpu.make_async_copy(
            source.at[:, pl.ds(at, cuts[sub])], weights[sub].at[2 * other + which], unit_sem.at[index]
        )

    def down_copy(index):
        at = pl.multiple_of(me_g * half + index * TILE_ROWS, TILE_ROWS)
        return pltpu.make_async_copy(
            down_hbm.at[pl.ds(at, TILE_ROWS), :], down.at[pl.ds(index * TILE_ROWS, TILE_ROWS), :], down_sem.at[index]
        )

    def table_copy(sub):
        piece = pl.ds(starts[sub], cuts[sub])
        return pltpu.make_async_copy(table_hbm.at[piece, :], table.at[piece, :], table_sem.at[sub])

    for index in range(min(RING, len(units))):
        unit_copy(index).start()
    for sub in range(count):
        table_copy(sub).start()

    barrier = pltpu.get_barrier_semaphore()
    for across, mask in others:
        pl.semaphore_signal(barrier, inc=1, device_id=token_peer(across, mask), device_id_type=MESH)
    for mask in (1, 2, 3):
        pl.semaphore_signal(barrier, inc=1, device_id={"hid": flip(me_h, mask)}, device_id_type=MESH)

    powers = lax.shift_left(jnp.ones_like(exps[...]), exps[...] + 10).astype(jnp.float32) * (2.0**-10)
    for block in range(blocks):
        at = block * LANES
        scale = powers[:, at // feats : at // feats + 1]
        fold[0, pl.ds(block * rows, rows), :] = codes[:, pl.ds(at, LANES)].astype(jnp.float32) * scale
    xrecv[0] = fold[0].astype(jnp.bfloat16)
    pl.semaphore_wait(barrier, 10)

    def feat_copy(across, mask):
        slot = 4 * across + mask
        return pltpu.make_async_remote_copy(
            src_ref=xrecv.at[0], dst_ref=xrecv.at[slot], send_sem=fs.at[slot - 1], recv_sem=fr.at[slot - 1],
            device_id=token_peer(across, mask), device_id_type=MESH,
        )

    for across, mask in others:
        feat_copy(across, mask).start()
    xfull[...] = jnp.zeros_like(xfull)
    for across, mask in others:
        feat_copy(across, mask).wait_recv()
    for across in range(2):
        for mask in range(4):
            fold[((me_g + across) % 2) * 4 + flip(me_f, mask)] = xrecv[4 * across + mask].astype(jnp.float32)
    for owner in range(2 * SPLIT):
        at = (owner // SPLIT) * PAD + (owner % SPLIT) * rows
        for block in range(blocks):
            xfull[pl.ds(at, rows), pl.ds(block * LANES, LANES)] = fold[owner, pl.ds(block * rows, rows), :]
    xmat[...] = xfull[...].astype(jnp.bfloat16)

    def core_copy(sub):
        return pltpu.make_async_remote_copy(
            src_ref=psend[sub], dst_ref=precv[sub], send_sem=ps.at[sub], recv_sem=pr.at[sub],
            device_id={"hid": flip(me_h, 1)}, device_id_type=MESH,
        )

    def chip_copy(sub):
        return pltpu.make_async_remote_copy(
            src_ref=xsend[sub], dst_ref=xgot[sub], send_sem=cs.at[sub], recv_sem=cr.at[sub],
            device_id={"hid": flip(me_h, 2)}, device_id_type=MESH,
        )

    def hidden_copy(sub, mask):
        return pltpu.make_async_remote_copy(
            src_ref=hall[sub].at[0], dst_ref=hall[sub].at[mask],
            send_sem=hs.at[sub * 3 + mask - 1], recv_sem=hr.at[sub * 3 + mask - 1],
            device_id={"ffn": flip(me_f, mask)}, device_id_type=MESH,
        )

    def pair_copy():
        return pltpu.make_async_remote_copy(
            src_ref=zpair.at[0], dst_ref=zpair.at[1], send_sem=ys.at[0], recv_sem=yr.at[0],
            device_id={"groups": 1 - me_g}, device_id_type=MESH,
        )

    def z_copy(mask):
        return pltpu.make_async_remote_copy(
            src_ref=zall.at[0], dst_ref=zall.at[mask], send_sem=zs.at[mask - 1], recv_sem=zr.at[mask - 1],
            device_id={"hid": flip(me_h, mask)}, device_id_type=MESH,
        )

    def out_copy(across, mask):
        slot = 4 * across + mask - 1
        return pltpu.make_async_remote_copy(
            src_ref=obuf.at[((me_x + me_g + across) % 2) * 4 + flip(me_f, mask)], dst_ref=orecv.at[slot],
            send_sem=os.at[slot], recv_sem=orr.at[slot],
            device_id=token_peer(across, mask), device_id_type=MESH,
        )

    def sum_cores(sub):
        core_copy(sub).wait_recv()
        for which in range(2):
            xsend[sub][which] = own[sub][which, 1 - me_x] + precv[sub][which, 1 - me_x]
        chip_copy(sub).start()

    def finish_hidden(sub):
        chip_copy(sub).wait_recv()
        piece = pl.ds(starts[sub], cuts[sub])
        sums = [own[sub][which, me_x] + precv[sub][which, me_x] + xgot[sub][which] for which in range(2)]
        gate = sums[0] * scales[0:1, piece]
        value = gate / (1.0 + jnp.exp(-gate)) * (sums[1] * scales[1:2, piece])
        padded = jnp.concatenate([value, jnp.zeros((FULL - PAD, cuts[sub]), jnp.float32)], axis=0)
        hall[sub][0] = padded.astype(jnp.bfloat16)
        for mask in (3, 2, 1):
            hidden_copy(sub, mask).start()

    def mix(sub):
        table_copy(sub).wait()
        total = hall[sub][0].astype(jnp.float32) * sign_of(me_f, me_f)
        for mask in (1, 2, 3):
            hidden_copy(sub, mask).wait_recv()
            total = total + hall[sub][mask].astype(jnp.float32) * sign_of(flip(me_f, mask), me_f)
        total = total[:PAD]
        high = total.astype(jnp.bfloat16).astype(jnp.float32)
        both = jnp.concatenate([high, total - high], axis=0).astype(jnp.bfloat16)
        mixed = jnp.dot(both, table[pl.ds(starts[sub], cuts[sub]), :], preferred_element_type=jnp.float32)
        mixed = mixed[:PAD] + mixed[PAD:]
        if sub == 0:
            zsum[...] = mixed
        else:
            zsum[...] += mixed

    down_next = 0
    for index, (sub, other, which) in enumerate(units):
        unit_copy(index).wait()
        value = jnp.dot(xmat[...], weights[sub][2 * other + which], preferred_element_type=jnp.float32)
        target = psend[sub] if other else own[sub]
        for group in range(2):
            target[which, group] = value[group * PAD : (group + 1) * PAD]
        if index + RING < len(units):
            unit_copy(index + RING).start()
        elif down_next < down_tiles:
            down_copy(down_next).start()
            down_next += 1
        if which == 1:
            if other:
                core_copy(sub).start()
                if sub >= 1:
                    finish_hidden(sub - 1)
            else:
                sum_cores(sub)
                if sub >= 1:
                    mix(sub - 1)
    while down_next < down_tiles:
        down_copy(down_next).start()
        down_next += 1
    finish_hidden(count - 1)
    mix(count - 1)

    spare = jnp.zeros((FULL - PAD, chunk), jnp.float32)
    zpair[0] = jnp.concatenate([zsum[...], spare], axis=0).astype(jnp.bfloat16)
    pair_copy().start()
    mine = zsum[...] * sign_of(me_g, me_g)
    pair_copy().wait_recv()
    mine = mine + zpair[1].astype(jnp.float32)[:PAD]
    zall[0] = jnp.concatenate([mine, spare], axis=0).astype(jnp.bfloat16)
    for mask in (3, 2, 1):
        z_copy(mask).start()
    for index in range(down_tiles):
        down_copy(index).wait()
    for mask in (1, 2, 3):
        z_copy(mask).wait_recv()
    for target in range(2):
        groups = []
        for far in range(2):
            total = zall[2 * far].astype(jnp.float32) * (sign_of(me_c, target) * norm)
            total = total + zall[2 * far + 1].astype(jnp.float32) * (sign_of(1 - me_c, target) * norm)
            groups.append(total[:PAD])
        rot[target] = jnp.concatenate(groups, axis=0).astype(jnp.bfloat16)

    @pl.loop(0, depth // 512)
    def _(tile):
        at = pl.ds(pl.multiple_of(tile * 512, 512), 512)
        total = jnp.zeros((2 * PAD, 512), jnp.float32)
        for target in range(2):
            total = total + jnp.dot(
                rot[target], down[pl.ds(target * chunk, chunk), at], preferred_element_type=jnp.float32
            )
        part[:, at] = total

    for owner in range(2 * SPLIT):
        at = (owner // SPLIT) * PAD + (owner % SPLIT) * rows
        for block in range(blocks):
            fold[owner, pl.ds(block * rows, rows), :] = part[pl.ds(at, rows), pl.ds(block * LANES, LANES)]
    obuf[...] = fold[...].astype(jnp.bfloat16)
    for across, mask in others:
        out_copy(across, mask).start()
    total = fold[((me_x + me_g) % 2) * 4 + me_f]
    for across, mask in others:
        out_copy(across, mask).wait_recv()
        total = total + orecv[4 * across + mask - 1].astype(jnp.float32)
    fold[0] = total
    for block in range(blocks):
        at = pl.ds(block * LANES, LANES)
        out[:, at] = (fold[0, pl.ds(block * rows, rows), :] * dscale[:, at]).astype(jnp.bfloat16)

    for across, mask in others:
        feat_copy(across, mask).wait_send()
        out_copy(across, mask).wait_send()
    pair_copy().wait_send()
    for mask in (1, 2, 3):
        z_copy(mask).wait_send()
        for sub in range(count):
            hidden_copy(sub, mask).wait_send()
    for sub in range(count):
        core_copy(sub).wait_send()
        chip_copy(sub).wait_send()


def fused_on_device(
    act_codes, act_exps, gate_codes, up_codes, down_codes, gate_scale, up_scale, down_scale
):
    rows, depth = act_codes.shape
    width = gate_codes.shape[1]
    chunk = width // SPLIT
    feats = depth // act_exps.shape[1]
    cuts = [blocks * LANES for blocks in cut_chunk(chunk // LANES)]
    count = len(cuts)
    norm = float(1.0 / np.sqrt(width * lax.axis_size("ffn")))
    table = jnp.asarray(
        np.kron(sylvester_table(chunk // ORDER), paley_table()).astype(np.float32), dtype=jnp.bfloat16
    )
    folded = rows * (depth // LANES)
    vmem = pl.BlockSpec(memory_space=pltpu.VMEM)
    hbm = pl.BlockSpec(memory_space=pl.ANY)
    f32, bf16 = jnp.float32, jnp.bfloat16
    half = width // GROUPS
    scratch = [
        pltpu.VMEM((chunk, chunk), bf16),
        pltpu.VMEM((half, depth), bf16),
        pltpu.VMEM((2 * SPLIT, folded, LANES), f32),
        pltpu.VMEM((2 * SPLIT, folded, LANES), bf16),
        pltpu.VMEM((2 * PAD, depth), f32),
        pltpu.VMEM((2 * PAD, depth), bf16),
        pltpu.VMEM((PAD, chunk), f32),
        pltpu.VMEM((2, FULL, chunk), bf16),
        pltpu.VMEM((SPLIT, FULL, chunk), bf16),
        pltpu.VMEM((2, 2 * PAD, chunk), bf16),
        pltpu.VMEM((2 * PAD, depth), f32),
        pltpu.VMEM((2 * SPLIT, folded, LANES), bf16),
        pltpu.VMEM((2 * SPLIT - 1, folded, LANES), bf16),
    ]
    scratch += [pltpu.VMEM((4, depth, cut), bf16) for cut in cuts]
    for _ in range(3):
        scratch += [pltpu.VMEM((2, 2, PAD, cut), f32) for cut in cuts]
    for _ in range(2):
        scratch += [pltpu.VMEM((2, PAD, cut), f32) for cut in cuts]
    scratch += [pltpu.VMEM((SPLIT, FULL, cut), bf16) for cut in cuts]
    dma = pltpu.SemaphoreType.DMA
    scratch += [dma((4 * count,)), dma((count,)), dma((half // TILE_ROWS,)), dma((7,)), dma((7,))]
    scratch += [dma((count,)) for _ in range(4)]
    scratch += [dma((3 * count,)) for _ in range(2)]
    scratch += [dma((1,)), dma((1,)), dma((3,)), dma((3,)), dma((7,)), dma((7,))]
    at = (2 * lax.axis_index("groups") + lax.axis_index("hid") % 2) * chunk
    scales = jnp.stack([lax.dynamic_slice(each, (at,), (chunk,)) for each in (gate_scale, up_scale)])
    return pl.pallas_call(
        functools.partial(layer_kernel, (rows, depth, width, feats, norm)),
        out_shape=jax.ShapeDtypeStruct((rows, depth), bf16),
        in_specs=[vmem, vmem, hbm, hbm, hbm, vmem, vmem, hbm],
        out_specs=vmem,
        scratch_shapes=scratch,
        compiler_params=pltpu.CompilerParams(
            collective_id=0, has_side_effects=True, vmem_limit_bytes=62 * 2**20
        ),
        cost_estimate=pl.CostEstimate(
            flops=6 * rows * SPLIT * depth * width, bytes_accessed=3 * depth * width, transcendentals=0
        ),
    )(
        act_codes, act_exps, gate_codes, up_codes, down_codes,
        scales, down_scale.reshape(1, depth), table,
    )


def solution(mesh):
    in_specs = (
        P(("groups", "ffn"), "hid"),
        P(("groups", "ffn"), "hid"),
        P("hid", "ffn"),
        P("hid", "ffn"),
        P("ffn", "hid"),
        P("ffn"),
        P("ffn"),
        P("hid"),
    )
    out_specs = P(("groups", "ffn"), "hid")
    square = mesh.shape["groups"] == GROUPS and mesh.shape["ffn"] == SPLIT and mesh.shape["hid"] == SPLIT
    return jax.shard_map(
        fused_on_device if square else on_device, mesh=mesh, in_specs=in_specs, out_specs=out_specs, check_vma=False
    )
```

```python
import functools

import jax
import jax.numpy as jnp
import numpy as np
from jax import lax
from jax.experimental import pallas as pl
from jax.experimental.pallas import tpu as pltpu
from jax.sharding import PartitionSpec as P

MESH = pl.DeviceIdType.MESH


def field_product(first, second):
    return (
        (first[0] * second[0] + 2 * first[1] * second[1]) % 5,
        (first[0] * second[1] + first[1] * second[0]) % 5,
    )


def paley_table():
    elements = [(alpha, beta) for alpha in range(5) for beta in range(5)]
    squares = set()
    for item in elements:
        if item != (0, 0):
            squares.add(field_product(item, item))
    jacobi = np.zeros((25, 25))
    for left in range(25):
        for right in range(25):
            diff = (
                (elements[left][0] - elements[right][0]) % 5,
                (elements[left][1] - elements[right][1]) % 5,
            )
            if diff == (0, 0):
                jacobi[left, right] = 0.0
            elif diff in squares:
                jacobi[left, right] = 1.0
            else:
                jacobi[left, right] = -1.0
    conference = np.zeros((26, 26))
    conference[0, 1:] = 1.0
    conference[1:, 0] = 1.0
    conference[1:, 1:] = jacobi
    return np.kron(conference, np.array([[1.0, -1.0], [-1.0, -1.0]])) + np.kron(
        np.eye(26), np.array([[1.0, 1.0], [1.0, -1.0]])
    )


def sylvester_table(order):
    table = np.ones((1, 1))
    while table.shape[0] < order:
        table = np.kron(table, np.array([[1.0, 1.0], [1.0, -1.0]]))
    return table


def activate(sums, gate_scale, up_scale, width):
    gate = sums[:, :width] * gate_scale
    up_val = sums[:, width:] * up_scale
    return (jax.nn.silu(gate) * up_val).astype(jnp.bfloat16)


def on_device(
    act_codes, act_exps, gate_codes, up_codes, down_codes, gate_scale, up_scale, down_scale
):
    row_count, col_count = act_codes.shape
    blocks = act_exps.shape[1]
    scales = jnp.exp2(act_exps.astype(jnp.float32))
    features = (
        (
            act_codes.reshape(row_count, blocks, col_count // blocks).astype(jnp.float32)
            * scales[:, :, None]
        )
        .reshape(row_count, col_count)
        .astype(jnp.bfloat16)
    )
    width = gate_codes.shape[1]
    piece = lax.all_gather(features, "ffn", axis=0, tiled=True)
    gate_part = jnp.dot(piece, gate_codes, preferred_element_type=jnp.float32)
    up_part = jnp.dot(piece, up_codes, preferred_element_type=jnp.float32)
    partial_sums = jnp.concatenate([gate_part, up_part], axis=1)
    summed = lax.psum(partial_sums, "hid")
    hidden = activate(summed, gate_scale, up_scale, width)
    parts = lax.axis_size("ffn")
    tokens = hidden.shape[0]
    per_dev = tokens // parts
    local = width // 52
    small_table = jnp.asarray(paley_table(), dtype=jnp.bfloat16)
    outer_table = jnp.asarray(sylvester_table(parts), dtype=jnp.float32)
    inner_table = jnp.asarray(sylvester_table(local), dtype=jnp.float32)
    norm_factor = 1.0 / np.sqrt(parts * width)
    grouped = hidden.reshape(parts, per_dev, width)
    block = lax.all_to_all(grouped, "ffn", split_axis=0, concat_axis=0, tiled=True)
    items = block.shape[1]
    cube = block.reshape(parts, items, local, 52)
    mixed = jnp.einsum("snli,ik->snlk", cube, small_table, preferred_element_type=jnp.float32)
    across = jnp.einsum("snlk,sS->Snlk", mixed, outer_table, precision=lax.Precision.HIGHEST)
    turned = jnp.einsum("Snlk,lL->SnLk", across, inner_table, precision=lax.Precision.HIGHEST)
    rotated = (turned * norm_factor).reshape(parts, items, width).astype(jnp.bfloat16)
    returned = lax.all_to_all(rotated, "ffn", split_axis=0, concat_axis=0, tiled=True)
    rotated_rows = returned.reshape(tokens, width)
    total = lax.psum_scatter(
        jnp.dot(rotated_rows, down_codes, preferred_element_type=jnp.float32),
        "ffn",
        scatter_dimension=0,
        tiled=True,
    )
    return (total * down_scale).astype(jnp.bfloat16)


LANES = 128
ORDER = 52
SPLIT = 4
TILE_ROWS = 256
GROUPS = 2
RING = 12
PAD = 24
FULL = 32


def flip(index, mask):
    if mask == 1:
        return index + 1 - 2 * (index % 2)
    if mask == 2:
        return (index + 2) % 4
    if mask == 3:
        return 3 - index
    return index


def sign_of(first, second):
    low = (first % 2) * (second % 2)
    high = (first // 2) * (second // 2)
    odd = (low + high) % 2
    return jnp.asarray(1 - 2 * odd, jnp.int32).astype(jnp.float32)


def cut_chunk(blocks):
    cuts = []
    while blocks > 5:
        cuts.append(4)
        blocks -= 4
    if blocks > 2:
        cuts += [blocks - 2, 2]
    else:
        cuts.append(blocks)
    return cuts


def layer_kernel(plan, *refs):
    rows, depth, width, feats, norm = plan
    chunk = width // SPLIT
    cuts = [blocks * LANES for blocks in cut_chunk(chunk // LANES)]
    starts = [sum(cuts[:index]) for index in range(len(cuts))]
    count = len(cuts)
    blocks = depth // LANES
    half = width // GROUPS
    down_tiles = half // TILE_ROWS
    refs = list(refs)
    (codes, exps, gate_hbm, up_hbm, down_hbm, gscale, uscale, dscale, table_hbm, out) = refs[:10]
    (table, down, fold, xrecv, xfull, xmat, zsum, zpair, zall, rot, part, obuf, orecv) = refs[10:23]
    weights, own, psend, precv, xsend, xgot, hall = [refs[23 + count * k : 23 + count * (k + 1)] for k in range(7)]
    (unit_sem, table_sem, down_sem, fs, fr, ps, pr, cs, cr, hs, hr, ys, yr, zs, zr, os, orr) = refs[23 + 7 * count :]
    me_g = lax.axis_index("groups")
    me_f = lax.axis_index("ffn")
    me_h = lax.axis_index("hid")
    me_x, me_c = me_h // 2, me_h % 2
    others = [(across, mask) for across in (1, 0) for mask in (3, 2, 1, 0) if across or mask]

    def token_peer(across, mask):
        return {"groups": (me_g + across) % 2, "ffn": flip(me_f, mask)}

    units = [(sub, other, which) for sub in range(count) for other in (1, 0) for which in (0, 1)]

    def unit_copy(index):
        sub, other, which = units[index]
        source = up_hbm if which else gate_hbm
        at = pl.multiple_of((2 * me_g + (me_c + other) % 2) * chunk + starts[sub], LANES)
        return pltpu.make_async_copy(
            source.at[:, pl.ds(at, cuts[sub])], weights[sub].at[2 * other + which], unit_sem.at[index]
        )

    def down_copy(index):
        at = pl.multiple_of(me_g * half + index * TILE_ROWS, TILE_ROWS)
        return pltpu.make_async_copy(
            down_hbm.at[pl.ds(at, TILE_ROWS), :], down.at[pl.ds(index * TILE_ROWS, TILE_ROWS), :], down_sem.at[index]
        )

    def table_copy(sub):
        piece = pl.ds(starts[sub], cuts[sub])
        return pltpu.make_async_copy(table_hbm.at[piece, :], table.at[piece, :], table_sem.at[sub])

    for index in range(min(RING, len(units))):
        unit_copy(index).start()
    for sub in range(count):
        table_copy(sub).start()

    barrier = pltpu.get_barrier_semaphore()
    for across, mask in others:
        pl.semaphore_signal(barrier, inc=1, device_id=token_peer(across, mask), device_id_type=MESH)
    for mask in (1, 2, 3):
        pl.semaphore_signal(barrier, inc=1, device_id={"hid": flip(me_h, mask)}, device_id_type=MESH)

    powers = lax.shift_left(jnp.ones_like(exps[...]), exps[...] + 10).astype(jnp.float32) * (2.0**-10)
    for block in range(blocks):
        at = block * LANES
        scale = powers[:, at // feats : at // feats + 1]
        fold[0, pl.ds(block * rows, rows), :] = codes[:, pl.ds(at, LANES)].astype(jnp.float32) * scale
    xrecv[0] = fold[0].astype(jnp.bfloat16)
    pl.semaphore_wait(barrier, 10)

    def feat_copy(across, mask):
        slot = 4 * across + mask
        return pltpu.make_async_remote_copy(
            src_ref=xrecv.at[0], dst_ref=xrecv.at[slot], send_sem=fs.at[slot - 1], recv_sem=fr.at[slot - 1],
            device_id=token_peer(across, mask), device_id_type=MESH,
        )

    for across, mask in others:
        feat_copy(across, mask).start()
    xfull[...] = jnp.zeros_like(xfull)
    for across, mask in others:
        feat_copy(across, mask).wait_recv()
    for across in range(2):
        for mask in range(4):
            fold[((me_g + across) % 2) * 4 + flip(me_f, mask)] = xrecv[4 * across + mask].astype(jnp.float32)
    for owner in range(2 * SPLIT):
        at = (owner // SPLIT) * PAD + (owner % SPLIT) * rows
        for block in range(blocks):
            xfull[pl.ds(at, rows), pl.ds(block * LANES, LANES)] = fold[owner, pl.ds(block * rows, rows), :]
    xmat[...] = xfull[...].astype(jnp.bfloat16)

    def core_copy(sub):
        return pltpu.make_async_remote_copy(
            src_ref=psend[sub], dst_ref=precv[sub], send_sem=ps.at[sub], recv_sem=pr.at[sub],
            device_id={"hid": flip(me_h, 1)}, device_id_type=MESH,
        )

    def chip_copy(sub):
        return pltpu.make_async_remote_copy(
            src_ref=xsend[sub], dst_ref=xgot[sub], send_sem=cs.at[sub], recv_sem=cr.at[sub],
            device_id={"hid": flip(me_h, 2)}, device_id_type=MESH,
        )

    def hidden_copy(sub, mask):
        return pltpu.make_async_remote_copy(
            src_ref=hall[sub].at[0], dst_ref=hall[sub].at[mask],
            send_sem=hs.at[sub * 3 + mask - 1], recv_sem=hr.at[sub * 3 + mask - 1],
            device_id={"ffn": flip(me_f, mask)}, device_id_type=MESH,
        )

    first = (chunk // LANES + 1) // 2 * LANES
    sides = ((0, first), (first, chunk - first))

    def pair_copy(side):
        piece = pl.ds(*sides[side])
        return pltpu.make_async_remote_copy(
            src_ref=zpair.at[0, :, piece], dst_ref=zpair.at[1, :, piece], send_sem=ys.at[side], recv_sem=yr.at[side],
            device_id={"groups": 1 - me_g}, device_id_type=MESH,
        )

    def z_copy(side, mask):
        piece = pl.ds(*sides[side])
        slot = 3 * side + mask - 1
        return pltpu.make_async_remote_copy(
            src_ref=zall.at[0, :, piece], dst_ref=zall.at[mask, :, piece], send_sem=zs.at[slot], recv_sem=zr.at[slot],
            device_id={"hid": flip(me_h, mask)}, device_id_type=MESH,
        )

    def out_copy(across, mask):
        slot = 4 * across + mask - 1
        return pltpu.make_async_remote_copy(
            src_ref=obuf.at[((me_x + me_g + across) % 2) * 4 + flip(me_f, mask)], dst_ref=orecv.at[slot],
            send_sem=os.at[slot], recv_sem=orr.at[slot],
            device_id=token_peer(across, mask), device_id_type=MESH,
        )

    def sum_cores(sub):
        core_copy(sub).wait_recv()
        for which in range(2):
            xsend[sub][which] = own[sub][which, 1 - me_x] + precv[sub][which, 1 - me_x]
        chip_copy(sub).start()

    def finish_hidden(sub):
        chip_copy(sub).wait_recv()
        at = pl.multiple_of((2 * me_g + me_c) * chunk + starts[sub], LANES)

        def column(ref):
            return ref[pl.ds(at, cuts[sub])].reshape(1, cuts[sub])

        sums = [own[sub][which, me_x] + precv[sub][which, me_x] + xgot[sub][which] for which in range(2)]
        gate = sums[0] * column(gscale)
        value = gate / (1.0 + jnp.exp(-gate)) * (sums[1] * column(uscale))
        padded = jnp.concatenate([value, jnp.zeros((FULL - PAD, cuts[sub]), jnp.float32)], axis=0)
        hall[sub][0] = padded.astype(jnp.bfloat16)
        for mask in (3, 2, 1):
            hidden_copy(sub, mask).start()

    def mix(sub):
        table_copy(sub).wait()
        total = hall[sub][0].astype(jnp.float32) * sign_of(me_f, me_f)
        for mask in (1, 2, 3):
            hidden_copy(sub, mask).wait_recv()
            total = total + hall[sub][mask].astype(jnp.float32) * sign_of(flip(me_f, mask), me_f)
        total = total[:PAD]
        high = total.astype(jnp.bfloat16).astype(jnp.float32)
        both = jnp.concatenate([high, total - high], axis=0).astype(jnp.bfloat16)
        mixed = jnp.dot(both, table[pl.ds(starts[sub], cuts[sub]), :], preferred_element_type=jnp.float32)
        mixed = mixed[:PAD] + mixed[PAD:]
        if sub == 0:
            zsum[...] = mixed
        else:
            zsum[...] += mixed

    down_next = 0
    for index, (sub, other, which) in enumerate(units):
        unit_copy(index).wait()
        value = jnp.dot(xmat[...], weights[sub][2 * other + which], preferred_element_type=jnp.float32)
        target = psend[sub] if other else own[sub]
        for group in range(2):
            target[which, group] = value[group * PAD : (group + 1) * PAD]
        if index + RING < len(units):
            unit_copy(index + RING).start()
        elif down_next < down_tiles:
            down_copy(down_next).start()
            down_next += 1
        if which == 1:
            if other:
                core_copy(sub).start()
                if sub >= 1:
                    finish_hidden(sub - 1)
            else:
                sum_cores(sub)
                if sub >= 1:
                    mix(sub - 1)
    while down_next < down_tiles:
        down_copy(down_next).start()
        down_next += 1
    finish_hidden(count - 1)
    mix(count - 1)

    for side, (at, wide) in enumerate(sides):
        spare = jnp.zeros((FULL - PAD, wide), jnp.float32)
        piece = pl.ds(at, wide)
        zpair[0, :, piece] = jnp.concatenate([zsum[:, piece], spare], axis=0).astype(jnp.bfloat16)
        pair_copy(side).start()
    for side, (at, wide) in enumerate(sides):
        spare = jnp.zeros((FULL - PAD, wide), jnp.float32)
        piece = pl.ds(at, wide)
        pair_copy(side).wait_recv()
        mine = zsum[:, piece] * sign_of(me_g, me_g) + zpair[1, :, piece].astype(jnp.float32)[:PAD]
        zall[0, :, piece] = jnp.concatenate([mine, spare], axis=0).astype(jnp.bfloat16)
        for mask in (3, 2, 1):
            z_copy(side, mask).start()
    for index in range(down_tiles):
        down_copy(index).wait()
    for side in range(2):
        for mask in (1, 2, 3):
            z_copy(side, mask).wait_recv()
    for target in range(2):
        groups = []
        for far in range(2):
            total = zall[2 * far].astype(jnp.float32) * (sign_of(me_c, target) * norm)
            total = total + zall[2 * far + 1].astype(jnp.float32) * (sign_of(1 - me_c, target) * norm)
            groups.append(total[:PAD])
        rot[target] = jnp.concatenate(groups, axis=0).astype(jnp.bfloat16)

    @pl.loop(0, depth // 512)
    def _(tile):
        at = pl.ds(pl.multiple_of(tile * 512, 512), 512)
        total = jnp.zeros((2 * PAD, 512), jnp.float32)
        for target in range(2):
            total = total + jnp.dot(
                rot[target], down[pl.ds(target * chunk, chunk), at], preferred_element_type=jnp.float32
            )
        part[:, at] = total

    for owner in range(2 * SPLIT):
        at = (owner // SPLIT) * PAD + (owner % SPLIT) * rows
        for block in range(blocks):
            fold[owner, pl.ds(block * rows, rows), :] = part[pl.ds(at, rows), pl.ds(block * LANES, LANES)]
    obuf[...] = fold[...].astype(jnp.bfloat16)
    for across, mask in others:
        out_copy(across, mask).start()
    total = fold[((me_x + me_g) % 2) * 4 + me_f]
    for across, mask in others:
        out_copy(across, mask).wait_recv()
        total = total + orecv[4 * across + mask - 1].astype(jnp.float32)
    fold[0] = total
    for block in range(blocks):
        at = pl.ds(block * LANES, LANES)
        out[:, at] = (fold[0, pl.ds(block * rows, rows), :] * dscale[:, at]).astype(jnp.bfloat16)

    for across, mask in others:
        feat_copy(across, mask).wait_send()
        out_copy(across, mask).wait_send()
    for side in range(2):
        pair_copy(side).wait_send()
        for mask in (1, 2, 3):
            z_copy(side, mask).wait_send()
    for mask in (1, 2, 3):
        for sub in range(count):
            hidden_copy(sub, mask).wait_send()
    for sub in range(count):
        core_copy(sub).wait_send()
        chip_copy(sub).wait_send()


def fused_on_device(
    act_codes, act_exps, gate_codes, up_codes, down_codes, gate_scale, up_scale, down_scale
):
    rows, depth = act_codes.shape
    width = gate_codes.shape[1]
    chunk = width // SPLIT
    feats = depth // act_exps.shape[1]
    cuts = [blocks * LANES for blocks in cut_chunk(chunk // LANES)]
    count = len(cuts)
    norm = float(1.0 / np.sqrt(width * lax.axis_size("ffn")))
    table = jnp.asarray(
        np.kron(sylvester_table(chunk // ORDER), paley_table()).astype(np.float32), dtype=jnp.bfloat16
    )
    folded = rows * (depth // LANES)
    vmem = pl.BlockSpec(memory_space=pltpu.VMEM)
    hbm = pl.BlockSpec(memory_space=pl.ANY)
    f32, bf16 = jnp.float32, jnp.bfloat16
    half = width // GROUPS
    scratch = [
        pltpu.VMEM((chunk, chunk), bf16),
        pltpu.VMEM((half, depth), bf16),
        pltpu.VMEM((2 * SPLIT, folded, LANES), f32),
        pltpu.VMEM((2 * SPLIT, folded, LANES), bf16),
        pltpu.VMEM((2 * PAD, depth), f32),
        pltpu.VMEM((2 * PAD, depth), bf16),
        pltpu.VMEM((PAD, chunk), f32),
        pltpu.VMEM((2, FULL, chunk), bf16),
        pltpu.VMEM((SPLIT, FULL, chunk), bf16),
        pltpu.VMEM((2, 2 * PAD, chunk), bf16),
        pltpu.VMEM((2 * PAD, depth), f32),
        pltpu.VMEM((2 * SPLIT, folded, LANES), bf16),
        pltpu.VMEM((2 * SPLIT - 1, folded, LANES), bf16),
    ]
    scratch += [pltpu.VMEM((4, depth, cut), bf16) for cut in cuts]
    for _ in range(3):
        scratch += [pltpu.VMEM((2, 2, PAD, cut), f32) for cut in cuts]
    for _ in range(2):
        scratch += [pltpu.VMEM((2, PAD, cut), f32) for cut in cuts]
    scratch += [pltpu.VMEM((SPLIT, FULL, cut), bf16) for cut in cuts]
    dma = pltpu.SemaphoreType.DMA
    scratch += [dma((4 * count,)), dma((count,)), dma((half // TILE_ROWS,)), dma((7,)), dma((7,))]
    scratch += [dma((count,)) for _ in range(4)]
    scratch += [dma((3 * count,)) for _ in range(2)]
    scratch += [dma((2,)), dma((2,)), dma((6,)), dma((6,)), dma((7,)), dma((7,))]
    return pl.pallas_call(
        functools.partial(layer_kernel, (rows, depth, width, feats, norm)),
        out_shape=jax.ShapeDtypeStruct((rows, depth), bf16),
        in_specs=[vmem, vmem, hbm, hbm, hbm, vmem, vmem, vmem, hbm],
        out_specs=vmem,
        scratch_shapes=scratch,
        compiler_params=pltpu.CompilerParams(
            collective_id=0, has_side_effects=True, vmem_limit_bytes=62 * 2**20
        ),
        cost_estimate=pl.CostEstimate(
            flops=6 * rows * SPLIT * depth * width, bytes_accessed=3 * depth * width, transcendentals=0
        ),
    )(
        act_codes, act_exps, gate_codes, up_codes, down_codes,
        gate_scale, up_scale, down_scale.reshape(1, depth), table,
    )


def solution(mesh):
    in_specs = (
        P(("groups", "ffn"), "hid"),
        P(("groups", "ffn"), "hid"),
        P("hid", "ffn"),
        P("hid", "ffn"),
        P("ffn", "hid"),
        P("ffn"),
        P("ffn"),
        P("hid"),
    )
    out_specs = P(("groups", "ffn"), "hid")
    square = mesh.shape["groups"] == GROUPS and mesh.shape["ffn"] == SPLIT and mesh.shape["hid"] == SPLIT
    return jax.shard_map(
        fused_on_device if square else on_device, mesh=mesh, in_specs=in_specs, out_specs=out_specs, check_vma=False
    )
```
